32 devices in a mesh: context: 16 (over z, y, x), fsdp: 2 (over core).
Axes of the slice: x: 2, y: 2, z: 4, core: 2. Of those that a mesh axis runs over, the one named last changes fastest.
Arguments:
- queries: bfloat16 [2, 2048, 2048], P('fsdp', 'context'), may hold values from -200 to 200, as said below
- keys: bfloat16 [2, 2048, 1024], P('fsdp', 'context'), may hold values from -20 to 20, as said below
- values: bfloat16 [2, 2048, 1024], P('fsdp', 'context'), may hold values from -6 to 6
- output_gradient: bfloat16 [2, 2048, 2048], P('fsdp', 'context'), may hold values from -48 to 48
- adapter_hidden: bfloat16 [2, 2048, 16], P('fsdp', 'context'), may hold values from -0.09375 to 0.09375
- counts: int32 [2, 16], P('fsdp', 'context'), may hold values from 112 to 128, as said below
- offsets: int32 [2, 16], P('fsdp', 'context'), may hold values from 0 to 1776, as said below
Outputs:
- grad_queries: bfloat16 [2, 2048, 2048], P('fsdp', 'context')
- grad_keys: bfloat16 [2, 2048, 1024], P('fsdp', 'context')
- value_gradient: bfloat16 [2, 2048, 1024], P('fsdp', 'context')
- adapter_grad: float32 [16, 1024], P(None, 'fsdp')
The draws below stay inside these ranges and needn't reach their ends.
Inputs may be any that keep to these rules, and one draw needn't show every extreme that they name: `counts`: A shard's valid tokens fill its first slots. In every row some shard is full, and 9 consecutive shards, not starting at the first shard, hold 112 valid tokens each. offsets[row, s] is the sum of counts[row, r] over r < s. `queries`: finite values. `keys`: finite values.
All inputs are finite; a program needn't handle non-finite values.
Results may differ from the reference program's by a relative error of at most 0.01.
Values may be sent and summed in bfloat16 or wider, within the bound.
A program may use at most 64 MiB of HBM per device.

```python
import jax
import jax.numpy as jnp
from jax import lax

HQ = 16
KEY_VALUE_HEADS = 8
HEAD_SIZE = 128
ADAPTER_RANK = 16
WINDOW = 1024
SHARD_TOKENS = 128
MIN_VALID = 112
REACH = 10
SEQUENCE_TOKENS = 2048
BATCH_SEQUENCES = 2


def draw_core(key):
    base_key = jax.random.fold_in(key, 7)
    key_first_part, key_second_part = jax.random.split(base_key, 2)
    shard_number = SEQUENCE_TOKENS // SHARD_TOKENS
    key_start_index = jnp.clip(jax.random.normal(key_first_part, (BATCH_SEQUENCES, shard_number, SHARD_TOKENS, KEY_VALUE_HEADS, HEAD_SIZE), jnp.float32), -6.0, 6.0)
    query_start_index = jnp.clip(jax.random.normal(key_second_part, (BATCH_SEQUENCES, shard_number, SHARD_TOKENS, KEY_VALUE_HEADS, 2, HEAD_SIZE), jnp.float32), -6.0, 6.0)
    key_results = key_start_index
    query_results = query_start_index
    return (key_results, query_results)


def draw_keys(key, part):
    key_results, query_results = draw_core(key)
    return key_results.reshape(BATCH_SEQUENCES, SEQUENCE_TOKENS, KEY_VALUE_HEADS * HEAD_SIZE).astype(jnp.bfloat16)


def draw_queries(key, part):
    key_results, query_results = draw_core(key)
    return query_results.reshape(BATCH_SEQUENCES, SEQUENCE_TOKENS, KEY_VALUE_HEADS * 2 * HEAD_SIZE).astype(jnp.bfloat16)


def count_table(key):
    shard_number = SEQUENCE_TOKENS // SHARD_TOKENS
    key_first_part, key_second_part = jax.random.split(jax.random.fold_in(key, 19))
    table = jax.random.randint(key_first_part, (BATCH_SEQUENCES, shard_number), MIN_VALID, SHARD_TOKENS + 1, jnp.int32)
    begin = jax.random.randint(key_second_part, (BATCH_SEQUENCES, 1), 1, shard_number - REACH + 1, jnp.int32)
    index = jnp.arange(shard_number, dtype=jnp.int32)[None, :]
    run_mask = (index >= begin) & (index < begin + REACH - 1)
    table = jnp.where(run_mask, MIN_VALID, table)
    table = jnp.where(index == (begin + REACH) % shard_number, SHARD_TOKENS, table)
    return table.astype(jnp.int32)


def draw_counts(key, part):
    return count_table(key)


def draw_offsets(key, part):
    table = count_table(key)
    return (jnp.cumsum(table, axis=1) - table).astype(jnp.int32)


def shard_levels(stream_key, extent, cuts, low, high):
    loudness, own = 1.0, jax.random.fold_in(stream_key, 6)
    for position, shards_of in cuts:
        heights = jnp.exp(jax.random.uniform(jax.random.fold_in(own, position), (shards_of,), jnp.float32, low / len(cuts), high / len(cuts)))
        loudness = loudness * jnp.repeat(heights, extent[position] // shards_of).reshape([-1 if axis == position else 1 for axis in range(len(extent))])
    return loudness


def normal_values(own_key, shape, scale, bound, pieces=(), kind=jnp.bfloat16):
    loudness = shard_levels(own_key, shape, pieces, -0.22, 0.18) if pieces else 1.0
    values = jax.random.normal(own_key, shape, jnp.float32) * scale * loudness
    return jnp.minimum(jnp.maximum(values, -bound), bound).astype(kind)


def setup_inputs(seed: int = 0) -> dict:
    key_of = jax.random.split(jax.random.key(seed), 8)
    queries = draw_queries(jax.random.fold_in(key_of[7], 71), 0)
    keys = draw_keys(jax.random.fold_in(key_of[7], 71), 0)
    values = normal_values(key_of[2], (BATCH_SEQUENCES, SEQUENCE_TOKENS, KEY_VALUE_HEADS * HEAD_SIZE), 1.0, 6.0, ((0, 2), (1, 16)))
    output_gradient = normal_values(key_of[3], (BATCH_SEQUENCES, SEQUENCE_TOKENS, HQ * HEAD_SIZE), 8.0, 48.0, ((0, 2), (1, 16)))
    adapter_hidden = normal_values(key_of[4], (BATCH_SEQUENCES, SEQUENCE_TOKENS, ADAPTER_RANK), (BATCH_SEQUENCES * SEQUENCE_TOKENS) ** -0.5, 0.09375, ((0, 2), (1, 16)))
    counts = draw_counts(jax.random.fold_in(key_of[7], 71), 0)
    offsets = draw_offsets(jax.random.fold_in(key_of[7], 71), 0)
    return dict(queries=queries, keys=keys, values=values, output_gradient=output_gradient, adapter_hidden=adapter_hidden, counts=counts, offsets=offsets)


SCORE_SCALE = 168.0 ** -0.5
ADAPTER_SCALE = 2.0


def shard_grads(query_blk, dout_blk, key_window_rows, value_window_rows, count_win, offset_win, own_count, own_offset):
    present_rows = query_blk.shape[0]
    window_span = key_window_rows.shape[0] * present_rows
    slot_ids = jnp.arange(present_rows, dtype=jnp.int32)
    valid_rows = slot_ids < own_count
    masked_scores = jnp.where(valid_rows[:, None, None, None], dout_blk, jnp.zeros_like(dout_blk))
    key_pos = (offset_win[:, None] + slot_ids[None, :]).reshape(window_span)
    key_ok = (slot_ids[None, :] < count_win[:, None]).reshape(window_span)
    key_idx = jnp.arange(window_span, dtype=jnp.int32)
    query_idx = REACH * present_rows + slot_ids
    query_pos = own_offset + slot_ids
    allowed = key_ok[None, :] & (key_idx[None, :] <= query_idx[:, None]) & (query_pos[:, None] - key_pos[None, :] < WINDOW)
    query_f = query_blk.astype(jnp.float32)
    masked_f = masked_scores.astype(jnp.float32)
    key_float_rows = key_window_rows.reshape(window_span, KEY_VALUE_HEADS, HEAD_SIZE).astype(jnp.float32)
    value_float_rows = value_window_rows.reshape(window_span, KEY_VALUE_HEADS, HEAD_SIZE).astype(jnp.float32)
    scores = jnp.einsum('tgjd,kgd->gjtk', query_f, key_float_rows) * SCORE_SCALE
    live_scores = jnp.where(allowed, scores, -jnp.inf)
    peak = jnp.max(live_scores, axis=-1)
    log_total = peak + jnp.log(jnp.sum(jnp.exp(live_scores - peak[..., None]), axis=-1))
    weights = jnp.where(allowed, jnp.exp(scores - log_total[..., None]), 0.0)
    half_weights = weights.astype(jnp.bfloat16)
    dprobs = jnp.einsum('tgjd,kgd->gjtk', masked_f, value_float_rows)
    row_delta = jnp.sum(weights * dprobs, axis=-1)
    dscores = (weights * (dprobs - row_delta[..., None])).astype(jnp.bfloat16)
    dscores_f = dscores.astype(jnp.float32)
    grad_q = (SCORE_SCALE * jnp.einsum('gjtk,kgd->tgjd', dscores_f, key_float_rows)).astype(jnp.bfloat16)
    key_part = (SCORE_SCALE * jnp.einsum('gjtk,tgjd->kgd', dscores_f, query_f)).astype(jnp.bfloat16)
    value_part = jnp.einsum('gjtk,tgjd->kgd', half_weights.astype(jnp.float32), masked_f).astype(jnp.bfloat16)
    output_shape = (key_window_rows.shape[0], present_rows, KEY_VALUE_HEADS * HEAD_SIZE)
    return grad_q, key_part.reshape(output_shape), value_part.reshape(output_shape)


def one_row(row_items):
    query_single_row, key_row, value_row, output_gradient_row, count_row, offset_row = row_items
    shard_number = count_row.shape[0]
    feature_columns = KEY_VALUE_HEADS * HEAD_SIZE
    query_shard = query_single_row.reshape(shard_number, SHARD_TOKENS, KEY_VALUE_HEADS, 2, HEAD_SIZE)
    output_gradient_shard = output_gradient_row.reshape(shard_number, SHARD_TOKENS, KEY_VALUE_HEADS, 2, HEAD_SIZE)
    lead_zero = jnp.zeros((REACH, SHARD_TOKENS, feature_columns), jnp.bfloat16)
    key_pad = jnp.concatenate([lead_zero, key_row.reshape(shard_number, SHARD_TOKENS, feature_columns)], axis=0)
    value_pad = jnp.concatenate([lead_zero, value_row.reshape(shard_number, SHARD_TOKENS, feature_columns)], axis=0)
    count_pad = jnp.concatenate([jnp.zeros((REACH,), jnp.int32), count_row.astype(jnp.int32)], axis=0)
    offset_pad = jnp.concatenate([jnp.zeros((REACH,), jnp.int32), offset_row.astype(jnp.int32)], axis=0)

    def one_shard(carry, shard_id):
        key_acc, value_acc = carry
        query_blk = lax.dynamic_index_in_dim(query_shard, shard_id, 0, keepdims=False)
        dout_blk = lax.dynamic_index_in_dim(output_gradient_shard, shard_id, 0, keepdims=False)
        key_window_rows = lax.dynamic_slice_in_dim(key_pad, shard_id, REACH + 1, 0)
        value_window_rows = lax.dynamic_slice_in_dim(value_pad, shard_id, REACH + 1, 0)
        count_win = lax.dynamic_slice_in_dim(count_pad, shard_id, REACH + 1, 0)
        offset_win = lax.dynamic_slice_in_dim(offset_pad, shard_id, REACH + 1, 0)
        own_count = lax.dynamic_index_in_dim(count_row, shard_id, 0, keepdims=False).astype(jnp.int32)
        own_offset = lax.dynamic_index_in_dim(offset_row, shard_id, 0, keepdims=False).astype(jnp.int32)
        grad_q, key_part, value_part = shard_grads(query_blk, dout_blk, key_window_rows, value_window_rows, count_win, offset_win, own_count, own_offset)
        old_keys = lax.dynamic_slice_in_dim(key_acc, shard_id, REACH + 1, 0)
        old_values = lax.dynamic_slice_in_dim(value_acc, shard_id, REACH + 1, 0)
        key_acc = lax.dynamic_update_slice_in_dim(key_acc, old_keys + key_part.astype(jnp.float32), shard_id, 0)
        value_acc = lax.dynamic_update_slice_in_dim(value_acc, old_values + value_part.astype(jnp.float32), shard_id, 0)
        return (key_acc, value_acc), grad_q

    start_acc = jnp.zeros((shard_number + REACH, SHARD_TOKENS, feature_columns), jnp.float32)
    (key_acc, value_acc), grad_q = lax.scan(one_shard, (start_acc, start_acc), jnp.arange(shard_number, dtype=jnp.int32))
    grad_keys = key_acc[REACH:].astype(jnp.bfloat16).reshape(shard_number * SHARD_TOKENS, feature_columns)
    value_gradient = value_acc[REACH:].astype(jnp.bfloat16).reshape(shard_number * SHARD_TOKENS, feature_columns)
    return grad_q.reshape(shard_number * SHARD_TOKENS, HQ * HEAD_SIZE), grad_keys, value_gradient


def reference(queries, keys, values, output_gradient, adapter_hidden, counts, offsets):
    grad_queries, grad_keys, value_gradient = lax.map(one_row, (queries, keys, values, output_gradient, counts, offsets))
    flattened_hidden = adapter_hidden.reshape(-1, ADAPTER_RANK)
    flattened_values = value_gradient.reshape(-1, KEY_VALUE_HEADS * HEAD_SIZE)
    adapter_grad = ADAPTER_SCALE * jnp.dot(flattened_hidden.T, flattened_values, preferred_element_type=jnp.float32)
    return grad_queries, grad_keys, value_gradient, adapter_grad
```

```python
import functools
import math

import jax
import jax.numpy as jnp
from jax import lax
from jax.experimental import pallas as pl
from jax.experimental.pallas import tpu as pltpu
from jax.sharding import PartitionSpec as P

HQ = 16
KEY_VALUE_HEADS = 8
HEAD_SIZE = 128
WINDOW = 1024
REACH = 10
ADAPTER_RANK = 16


SCORE_SCALE = 168.0 ** (-0.5)
ADAPTER_SCALE = 2.0


def shifted(value, axis, steps):
    count = lax.axis_size(axis)
    initial, last = (max(0, -steps), min(count, count - steps))
    return lax.ppermute(value, axis, [(source, source + steps) for source in range(initial, last)])


def local(queries, keys, values, output_gradient, adapter_hidden, counts, offsets):
    present_rows = queries.shape[1]
    feature_columns = keys.shape[2]
    slot_ids = jnp.arange(present_rows, dtype=jnp.int32)
    own_offset = offsets[0, 0]
    own_count = counts[0, 0]
    valid_rows = slot_ids < own_count
    masked_scores = jnp.where(
        valid_rows[:, None], output_gradient[0], jnp.zeros_like(output_gradient[0])
    )
    query_quad_rows = queries[0].reshape(present_rows, KEY_VALUE_HEADS, 2, HEAD_SIZE)
    masked_quad_scores = masked_scores.reshape(present_rows, KEY_VALUE_HEADS, 2, HEAD_SIZE)
    own_items = (keys[0], values[0], offsets[0], counts[0])
    arrived = []
    current = own_items
    for hop_index in range(REACH):
        current = shifted((current[0], current[1], current[2], current[3]), "context", 1)
        arrived.append(current)
    window_items = arrived[::-1] + [own_items]
    key_complete = jnp.concatenate([shard_data[0] for shard_data in window_items], axis=0)
    value_complete = jnp.concatenate([shard_data[1] for shard_data in window_items], axis=0)
    key_pos = jnp.concatenate([shard_data[2][0] + slot_ids for shard_data in window_items], axis=0)
    key_ok = jnp.concatenate([slot_ids < shard_data[3][0] for shard_data in window_items], axis=0)
    total_keys = key_complete.shape[0]
    key_idx = jnp.arange(total_keys, dtype=jnp.int32)
    query_idx = REACH * present_rows + slot_ids
    query_pos = own_offset + slot_ids
    block_cap = 512
    block_list = []
    block_begin = 0
    while block_begin < total_keys:
        block_extent = min(block_cap, total_keys - block_begin)
        block_list.append((block_begin, block_extent))
        block_begin = block_begin + block_extent

    def block_scores(block_opening, block_extent):
        key_piece = key_complete[block_opening : block_opening + block_extent].reshape(
            block_extent, KEY_VALUE_HEADS, HEAD_SIZE
        )
        value_piece = value_complete[block_opening : block_opening + block_extent].reshape(
            block_extent, KEY_VALUE_HEADS, HEAD_SIZE
        )
        scores = (
            jnp.einsum(
                "tgjd,kgd->gjtk", query_quad_rows, key_piece, preferred_element_type=jnp.float32
            )
            * SCORE_SCALE
        )
        dprobs = jnp.einsum(
            "tgjd,kgd->gjtk", masked_quad_scores, value_piece, preferred_element_type=jnp.float32
        )
        return (scores, dprobs)

    statistic_shape = (KEY_VALUE_HEADS, 2, present_rows)
    stats = (
        jnp.full(statistic_shape, -1e30, jnp.float32),
        jnp.zeros(statistic_shape, jnp.float32),
        jnp.zeros(statistic_shape, jnp.float32),
    )
    allowed_list = []
    for block_opening, block_extent in block_list:
        tile_pos = key_pos[block_opening : block_opening + block_extent]
        tile_ok = key_ok[block_opening : block_opening + block_extent]
        tile_idx = key_idx[block_opening : block_opening + block_extent]
        allowed = (
            tile_ok[None, :]
            & (tile_idx[None, :] <= query_idx[:, None])
            & (query_pos[:, None] - tile_pos[None, :] < WINDOW)
        )
        allowed_list.append(allowed)
        first_running_max, first_running_sum, first_running_dot = stats
        first_scores, first_dprobs = block_scores(block_opening, block_extent)
        live_scores = jnp.where(allowed, first_scores, -jnp.inf)
        new_max = jnp.maximum(first_running_max, jnp.max(live_scores, axis=-1))
        rescale = jnp.exp(first_running_max - new_max)
        weights = jnp.exp(live_scores - new_max[..., None])
        stats = (
            new_max,
            first_running_sum * rescale + jnp.sum(weights, axis=-1),
            first_running_dot * rescale + jnp.sum(weights * first_dprobs, axis=-1),
        )
    running_max, running_sum, running_dot = stats
    log_total = running_max + jnp.log(running_sum)
    row_delta = running_dot / running_sum
    query_accumulator = jnp.zeros((present_rows, KEY_VALUE_HEADS, 2, HEAD_SIZE), jnp.float32)
    key_blocks = []
    value_blocks = []
    for block_number in range(len(block_list)):
        block_opening, block_extent = block_list[block_number]
        allowed = allowed_list[block_number]
        second_key_piece = key_complete[block_opening : block_opening + block_extent].reshape(
            block_extent, KEY_VALUE_HEADS, HEAD_SIZE
        )
        second_scores, second_dprobs = block_scores(block_opening, block_extent)
        second_weights = jnp.where(allowed, jnp.exp(second_scores - log_total[..., None]), 0.0)
        half_weights = second_weights.astype(jnp.bfloat16)
        dscores = (second_weights * (second_dprobs - row_delta[..., None])).astype(jnp.bfloat16)
        query_part = jnp.einsum(
            "gjtk,kgd->tgjd", dscores, second_key_piece, preferred_element_type=jnp.float32
        )
        key_part = (
            jnp.einsum(
                "gjtk,tgjd->kgd", dscores, query_quad_rows, preferred_element_type=jnp.float32
            )
            * SCORE_SCALE
        ).astype(jnp.bfloat16)
        value_part = jnp.einsum(
            "gjtk,tgjd->kgd", half_weights, masked_quad_scores, preferred_element_type=jnp.float32
        ).astype(jnp.bfloat16)
        query_part, key_part, value_part = (
            query_part,
            key_part.reshape(block_extent, feature_columns),
            value_part.reshape(block_extent, feature_columns),
        )
        query_accumulator = query_accumulator + query_part
        key_blocks.append(key_part)
        value_blocks.append(value_part)
    key_terms = jnp.concatenate(key_blocks, axis=0).reshape(
        REACH + 1, present_rows, feature_columns
    )
    value_terms = jnp.concatenate(value_blocks, axis=0).reshape(
        REACH + 1, present_rows, feature_columns
    )
    key_sum = key_terms[REACH].astype(jnp.float32)
    value_sum = value_terms[REACH].astype(jnp.float32)
    for distance in range(1, REACH + 1):
        back_keys, back_values = shifted(
            (key_terms[REACH - distance], value_terms[REACH - distance]), "context", -distance
        )
        key_sum = key_sum + back_keys.astype(jnp.float32)
        value_sum = value_sum + back_values.astype(jnp.float32)
    grad_keys = key_sum.astype(jnp.bfloat16)
    value_gradient = value_sum.astype(jnp.bfloat16)
    grad_queries = (
        (query_accumulator * SCORE_SCALE)
        .astype(jnp.bfloat16)
        .reshape(1, present_rows, HQ * HEAD_SIZE)
    )
    adapter_term = ADAPTER_SCALE * jnp.einsum(
        "ud,ug->dg", adapter_hidden[0], value_gradient, preferred_element_type=jnp.float32
    )
    adapter_whole = lax.psum(adapter_term, "context")
    adapter_grad = lax.psum_scatter(adapter_whole, "fsdp", scatter_dimension=1, tiled=True)
    return (grad_queries, grad_keys[None], value_gradient[None], adapter_grad)


MESH = pl.DeviceIdType.MESH
T = 128
D = HEAD_SIZE
EXP2_SCALE = SCORE_SCALE * math.log2(math.e)
SIDE_ROWS = 24


def lower_shard(block):
    return max(0, 2 * block - REACH)


def cols(index):
    return pl.ds(pl.multiple_of(index * D, D), D)


def head_kernel(
    shards, side_ref, k_ref, v_ref, q_ref, do_ref,
    dq_out, kv_out, ad_out,
    sbuf, kbuf, vbuf, qbuf, dobuf, ktbuf, pbuf, acc, rx, fin, dqbuf, adpart, adbuf,
    s_send, s_recv, k_send, k_recv, v_send, v_recv, q_send, q_recv, do_send, do_recv,
    fk_send, fv_send, x_send, x_recv, dq_send, dq_recv, kv_send, kv_recv, ad_send, ad_recv,
):
    me = lax.axis_index("context")
    core = lax.axis_index("fsdp")
    other = 1 - core
    row = me // KEY_VALUE_HEADS
    head = me % KEY_VALUE_HEADS
    blocks = shards // 2

    def is_self(chip, dev):
        return jnp.logical_and(chip == me, dev == core)

    def remote(src, dst, ssem, rsem, chip, dev):
        return pltpu.make_async_remote_copy(
            src_ref=src, dst_ref=dst, send_sem=ssem, recv_sem=rsem,
            device_id={"context": chip, "fsdp": dev}, device_id_type=MESH,
        )

    def send(src, dst, ssem, rsem, chip, dev):
        mine = is_self(chip, dev)

        @pl.when(mine)
        def _():
            pltpu.make_async_copy(src, dst, rsem).start()

        @pl.when(jnp.logical_not(mine))
        def _():
            remote(src, dst, ssem, rsem, chip, dev).start()

    def sent(src, dst, ssem, rsem, chip, dev):
        @pl.when(jnp.logical_not(is_self(chip, dev)))
        def _():
            remote(src, dst, ssem, rsem, chip, dev).wait_send()

    def arrived(dst, rsem):
        pltpu.make_async_copy(dst, dst, rsem).wait()

    barrier = pltpu.get_barrier_semaphore()

    def greet(step, carry):
        chip = lax.rem(me + step, shards)

        @pl.when(step > 0)
        def _():
            pl.semaphore_signal(
                barrier, inc=1, device_id={"context": chip, "fsdp": core}, device_id_type=MESH
            )

        pl.semaphore_signal(
            barrier, inc=1, device_id={"context": chip, "fsdp": other}, device_id_type=MESH
        )
        return carry

    lax.fori_loop(0, shards, greet, 0)
    pl.semaphore_wait(barrier, 2 * shards - 1)

    def target(step):
        kv_head = lax.rem(step + me, KEY_VALUE_HEADS)
        return kv_head, core * KEY_VALUE_HEADS + kv_head

    def side_args(step, dev):
        kv_head, chip = target(step)
        return side_ref, sbuf.at[me], s_send.at[kv_head, dev], s_recv.at[me], chip, dev

    def k_args(step):
        kv_head, chip = target(step)
        return k_ref.at[:, cols(kv_head)], kbuf.at[me], k_send.at[kv_head], k_recv.at[me], chip, me % 2

    def v_args(step):
        kv_head, chip = target(step)
        return v_ref.at[:, cols(kv_head)], vbuf.at[me], v_send.at[kv_head], v_recv.at[me], chip, me % 2

    def q_args(step, dev):
        kv_head, chip = target(step)
        return (q_ref.at[:, cols(2 * kv_head + dev)], qbuf.at[me], q_send.at[kv_head, dev],
                q_recv.at[me], chip, dev)

    def do_args(step, dev):
        kv_head, chip = target(step)
        return (do_ref.at[:, cols(2 * kv_head + dev)], dobuf.at[me], do_send.at[kv_head, dev],
                do_recv.at[me], chip, dev)

    def loop(count, body):
        def step_fn(step, carry):
            body(step)
            return carry
        lax.fori_loop(0, count, step_fn, 0)

    def first(act):
        def body(step):
            act(*k_args(step))
            act(*v_args(step))
            act(*side_args(step, 0))
            act(*side_args(step, 1))
        return body

    def second(act):
        def body(step):
            act(*q_args(step, 0))
            act(*q_args(step, 1))
        return body

    def third(act):
        def body(step):
            act(*do_args(step, 0))
            act(*do_args(step, 1))
        return body

    loop(KEY_VALUE_HEADS, first(send))
    loop(KEY_VALUE_HEADS, second(send))
    loop(KEY_VALUE_HEADS, third(send))

    acc[...] = jnp.zeros_like(acc)

    def forward(step):
        shard = 2 * step + core
        arrived(kbuf.at[shard], k_recv.at[shard])
        remote(kbuf.at[shard], kbuf.at[shard], fk_send.at[shard], k_recv.at[shard], me, other).start()
        arrived(vbuf.at[shard], v_recv.at[shard])
        remote(vbuf.at[shard], vbuf.at[shard], fv_send.at[shard], v_recv.at[shard], me, other).start()

    loop(blocks, forward)

    def from_sibling(step):
        shard = 2 * step + other
        arrived(kbuf.at[shard], k_recv.at[shard])
        arrived(vbuf.at[shard], v_recv.at[shard])

    loop(blocks, from_sibling)

    def side_in(step):
        arrived(sbuf.at[step], s_recv.at[step])

    loop(shards, side_in)

    slot = lax.broadcasted_iota(jnp.int32, (T, 2 * T), 0).astype(jnp.float32)
    lane = lax.broadcasted_iota(jnp.int32, (1, T), 1).astype(jnp.float32)
    starts = []
    total = 0
    for block in range(blocks):
        starts.append(total)
        total += (2 * block + 2 - lower_shard(block)) * T

    def dot(a, b, dims):
        return lax.dot_general(a, b, (dims, ((), ())), preferred_element_type=jnp.float32)

    for shard in range(shards):
        ktbuf[:, shard * T : (shard + 1) * T] = kbuf[shard].T

    for block in range(blocks):
        low, high = lower_shard(block), 2 * block + 2
        span = (high - low) * T
        arrived(qbuf.at[2 * block], q_recv.at[2 * block])
        arrived(qbuf.at[2 * block + 1], q_recv.at[2 * block + 1])
        q = qbuf[2 * block : 2 * block + 2].reshape(2 * T, D)
        k = kbuf[low:high].reshape(span, D)
        raw = dot(k, q, ((1,), (1,)))
        q_pos = jnp.concatenate(
            [sbuf[2 * block, 17:18, :] + lane, sbuf[2 * block + 1, 17:18, :] + lane], axis=1
        )
        q_index = jnp.concatenate([lane, lane + T], axis=1)
        pieces = []
        for shard in range(low, high):
            count = sbuf[shard, 16:17, :]
            top = jnp.concatenate([count, count], axis=1) - 1.0
            if shard >= 2 * block:
                top = jnp.minimum(top, q_index - (shard - 2 * block) * T)
            allowed = slot <= top
            if (high - shard) * T > WINDOW:
                offset = sbuf[shard, 17:18, :]
                bottom = q_pos - jnp.concatenate([offset, offset], axis=1) - WINDOW
                allowed = jnp.logical_and(allowed, slot > bottom)
            piece = raw[(shard - low) * T : (shard - low + 1) * T] * EXP2_SCALE
            pieces.append(jnp.where(allowed, piece, -1e30))
        peak = pieces[0].max(axis=0, keepdims=True)
        for piece in pieces[1:]:
            peak = jnp.maximum(peak, piece.max(axis=0, keepdims=True))
        weights = [jnp.exp2(piece - peak) for piece in pieces]
        norm = weights[0].sum(axis=0, keepdims=True)
        for weight in weights[1:]:
            norm = norm + weight.sum(axis=0, keepdims=True)
        inverse = 1.0 / norm
        for number, weight in enumerate(weights):
            begin = starts[block] + number * T
            pbuf[begin : begin + T, :] = weight * inverse

    def swap_args(block):
        return (acc.at[other, pl.ds(2 * T * block, 2 * T)], rx.at[block], x_send.at[block],
                x_recv.at[block], me, other)

    def dq_args(shard):
        return (dqbuf.at[shard], dq_out.at[:, cols(2 * head + core)], dq_send.at[shard],
                dq_recv.at[2 * head + core], shard, row)

    def kv_args(shard):
        return (fin.at[shard], kv_out.at[core, :, cols(head)], kv_send.at[shard],
                kv_recv.at[core, head], shard, row)

    factor = jnp.where(core == 0, SCORE_SCALE, 1.0).astype(jnp.float32)
    adapter = jnp.zeros((ADAPTER_RANK, D), jnp.float32)

    def finish(block, adapter):
        arrived(rx.at[block], x_recv.at[block])
        whole = acc[core, pl.ds(2 * T * block, 2 * T), :] + rx[block]
        half = (whole * factor).astype(jnp.bfloat16)
        for part in range(2):
            shard = 2 * block + part
            fin[shard] = half[part * T : (part + 1) * T]
            send(*kv_args(shard))
            hidden = sbuf[shard, 0:ADAPTER_RANK, :].astype(jnp.bfloat16)
            adapter = adapter + dot(hidden, half[part * T : (part + 1) * T], ((1,), (0,)))
        return adapter

    for block in reversed(range(blocks)):
        low, high = lower_shard(block), 2 * block + 2
        span = (high - low) * T
        grads = []
        for shard in (2 * block, 2 * block + 1):
            arrived(dobuf.at[shard], do_recv.at[shard])
            count = sbuf[shard, 16:17, :]
            grads.append(jnp.where(slot[:, :D] < count, dobuf[shard].astype(jnp.float32), 0.0))
        grad = jnp.concatenate(grads, axis=0).astype(jnp.bfloat16)
        q = qbuf[2 * block : 2 * block + 2].reshape(2 * T, D)
        v = vbuf[low:high].reshape(span, D)
        probs = pbuf[starts[block] : starts[block] + span, :]
        dprobs = dot(v, grad, ((1,), (1,)))
        delta = jnp.sum(probs * dprobs, axis=0, keepdims=True)
        dscores = (probs * (dprobs - delta)).astype(jnp.bfloat16)
        dq = dot(ktbuf[:, low * T : high * T], dscores, ((1,), (0,))).T * SCORE_SCALE
        dqbuf[2 * block] = dq[:T].astype(jnp.bfloat16)
        dqbuf[2 * block + 1] = dq[T:].astype(jnp.bfloat16)
        send(*dq_args(2 * block))
        send(*dq_args(2 * block + 1))
        acc[0, low * T : high * T, :] += dot(dscores, q, ((1,), (0,)))
        acc[1, low * T : high * T, :] += dot(probs.astype(jnp.bfloat16), grad, ((1,), (0,)))
        remote(*swap_args(block)).start()
        if block + 1 < blocks:
            adapter = finish(block + 1, adapter)
    adapter = finish(0, adapter)
    adpart[...] = adapter * ADAPTER_SCALE

    half_heads = KEY_VALUE_HEADS // 2

    def ad_args(step):
        chip = lax.rem(me + step, shards)
        return (adpart, adbuf.at[row, :, cols(head % half_heads)], ad_send.at[step],
                ad_recv.at[row, head % half_heads], chip, head // half_heads)

    @pl.when(core == 1)
    def _():
        loop(shards, lambda step: send(*ad_args(step)))

    loop(KEY_VALUE_HEADS, first(sent))
    loop(KEY_VALUE_HEADS, second(sent))
    loop(KEY_VALUE_HEADS, third(sent))

    def forward_sent(step):
        shard = 2 * step + core
        remote(kbuf.at[shard], kbuf.at[shard], fk_send.at[shard], k_recv.at[shard], me, other).wait_send()
        remote(vbuf.at[shard], vbuf.at[shard], fv_send.at[shard], v_recv.at[shard], me, other).wait_send()

    loop(blocks, forward_sent)
    for block in range(blocks):
        remote(*swap_args(block)).wait_send()
    loop(shards, lambda shard: sent(*dq_args(shard)))
    loop(shards, lambda shard: sent(*kv_args(shard)))

    @pl.when(core == 1)
    def _():
        loop(shards, lambda step: sent(*ad_args(step)))

    loop(HQ, lambda index: arrived(dq_out.at[:, cols(index)], dq_recv.at[index]))
    for kind in range(2):
        loop(KEY_VALUE_HEADS, lambda index: arrived(kv_out.at[kind, :, cols(index)], kv_recv.at[kind, index]))
    for source in range(2):
        for index in range(half_heads):
            arrived(adbuf.at[source, :, index * D : (index + 1) * D], ad_recv.at[source, index])
    ad_out[...] = adbuf[0] + adbuf[1]


def by_head(shards, queries, keys, values, output_gradient, adapter_hidden, counts, offsets):
    blocks = shards // 2
    total = sum((2 * block + 2 - lower_shard(block)) * T for block in range(blocks))
    side = jnp.concatenate(
        [
            adapter_hidden[0].astype(jnp.float32).T,
            jnp.broadcast_to(counts.astype(jnp.float32), (1, T)),
            jnp.broadcast_to(offsets.astype(jnp.float32), (1, T)),
            jnp.zeros((SIDE_ROWS - ADAPTER_RANK - 2, T), jnp.float32),
        ],
        axis=0,
    )
    bf16, f32 = jnp.bfloat16, jnp.float32
    dma = pltpu.SemaphoreType.DMA
    anywhere = pl.BlockSpec(memory_space=pl.ANY)
    vmem = pl.BlockSpec(memory_space=pltpu.VMEM)
    dq, kv, adapter = pl.pallas_call(
        functools.partial(head_kernel, shards),
        out_shape=(
            jax.ShapeDtypeStruct((T, HQ * D), bf16),
            jax.ShapeDtypeStruct((2, T, KEY_VALUE_HEADS * D), bf16),
            jax.ShapeDtypeStruct((ADAPTER_RANK, KEY_VALUE_HEADS * D // 2), f32),
        ),
        in_specs=[anywhere] * 5,
        out_specs=(anywhere, anywhere, vmem),
        scratch_shapes=[
            pltpu.VMEM((shards, SIDE_ROWS, T), f32),
            pltpu.VMEM((shards, T, D), bf16),
            pltpu.VMEM((shards, T, D), bf16),
            pltpu.VMEM((shards, T, D), bf16),
            pltpu.VMEM((shards, T, D), bf16),
            pltpu.VMEM((D, shards * T), bf16),
            pltpu.VMEM((total, 2 * T), f32),
            pltpu.VMEM((2, shards * T, D), f32),
            pltpu.VMEM((blocks, 2 * T, D), f32),
            pltpu.VMEM((shards, T, D), bf16),
            pltpu.VMEM((shards, T, D), bf16),
            pltpu.VMEM((ADAPTER_RANK, D), f32),
            pltpu.VMEM((2, ADAPTER_RANK, KEY_VALUE_HEADS * D // 2), f32),
            dma((KEY_VALUE_HEADS, 2)), dma((shards,)),
            dma((KEY_VALUE_HEADS,)), dma((shards,)),
            dma((KEY_VALUE_HEADS,)), dma((shards,)),
            dma((KEY_VALUE_HEADS, 2)), dma((shards,)),
            dma((KEY_VALUE_HEADS, 2)), dma((shards,)),
            dma((shards,)), dma((shards,)),
            dma((blocks,)), dma((blocks,)),
            dma((shards,)), dma((HQ,)),
            dma((shards,)), dma((2, KEY_VALUE_HEADS)),
            dma((shards,)), dma((2, KEY_VALUE_HEADS // 2)),
        ],
        compiler_params=pltpu.CompilerParams(
            collective_id=0, has_side_effects=True, vmem_limit_bytes=48 * 1024 * 1024
        ),
    )(side, keys[0], values[0], queries[0], output_gradient[0])
    return dq[None], kv[0][None], kv[1][None], adapter


def solution(mesh):
    shards = mesh.shape["context"]
    fits = shards == 2 * KEY_VALUE_HEADS and mesh.shape["fsdp"] == 2
    body = functools.partial(by_head, shards) if fits else local
    in_specs = (
        P("fsdp", "context", None),
        P("fsdp", "context", None),
        P("fsdp", "context", None),
        P("fsdp", "context", None),
        P("fsdp", "context", None),
        P("fsdp", "context"),
        P("fsdp", "context"),
    )
    out_specs = (
        P("fsdp", "context", None),
        P("fsdp", "context", None),
        P("fsdp", "context", None),
        P(None, "fsdp"),
    )
    return jax.shard_map(body, mesh=mesh, in_specs=in_specs, out_specs=out_specs, check_vma=False)
```

```python
import functools
import math

import jax
import jax.numpy as jnp
from jax import lax
from jax.experimental import pallas as pl
from jax.experimental.pallas import tpu as pltpu
from jax.sharding import PartitionSpec as P

HQ = 16
KEY_VALUE_HEADS = 8
HEAD_SIZE = 128
WINDOW = 1024
REACH = 10
ADAPTER_RANK = 16


SCORE_SCALE = 168.0 ** (-0.5)
ADAPTER_SCALE = 2.0


def shifted(value, axis, steps):
    count = lax.axis_size(axis)
    initial, last = (max(0, -steps), min(count, count - steps))
    return lax.ppermute(value, axis, [(source, source + steps) for source in range(initial, last)])


def local(queries, keys, values, output_gradient, adapter_hidden, counts, offsets):
    present_rows = queries.shape[1]
    feature_columns = keys.shape[2]
    slot_ids = jnp.arange(present_rows, dtype=jnp.int32)
    own_offset = offsets[0, 0]
    own_count = counts[0, 0]
    valid_rows = slot_ids < own_count
    masked_scores = jnp.where(
        valid_rows[:, None], output_gradient[0], jnp.zeros_like(output_gradient[0])
    )
    query_quad_rows = queries[0].reshape(present_rows, KEY_VALUE_HEADS, 2, HEAD_SIZE)
    masked_quad_scores = masked_scores.reshape(present_rows, KEY_VALUE_HEADS, 2, HEAD_SIZE)
    own_items = (keys[0], values[0], offsets[0], counts[0])
    arrived = []
    current = own_items
    for hop_index in range(REACH):
        current = shifted((current[0], current[1], current[2], current[3]), "context", 1)
        arrived.append(current)
    window_items = arrived[::-1] + [own_items]
    key_complete = jnp.concatenate([shard_data[0] for shard_data in window_items], axis=0)
    value_complete = jnp.concatenate([shard_data[1] for shard_data in window_items], axis=0)
    key_pos = jnp.concatenate([shard_data[2][0] + slot_ids for shard_data in window_items], axis=0)
    key_ok = jnp.concatenate([slot_ids < shard_data[3][0] for shard_data in window_items], axis=0)
    total_keys = key_complete.shape[0]
    key_idx = jnp.arange(total_keys, dtype=jnp.int32)
    query_idx = REACH * present_rows + slot_ids
    query_pos = own_offset + slot_ids
    block_cap = 512
    block_list = []
    block_begin = 0
    while block_begin < total_keys:
        block_extent = min(block_cap, total_keys - block_begin)
        block_list.append((block_begin, block_extent))
        block_begin = block_begin + block_extent

    def block_scores(block_opening, block_extent):
        key_piece = key_complete[block_opening : block_opening + block_extent].reshape(
            block_extent, KEY_VALUE_HEADS, HEAD_SIZE
        )
        value_piece = value_complete[block_opening : block_opening + block_extent].reshape(
            block_extent, KEY_VALUE_HEADS, HEAD_SIZE
        )
        scores = (
            jnp.einsum(
                "tgjd,kgd->gjtk", query_quad_rows, key_piece, preferred_element_type=jnp.float32
            )
            * SCORE_SCALE
        )
        dprobs = jnp.einsum(
            "tgjd,kgd->gjtk", masked_quad_scores, value_piece, preferred_element_type=jnp.float32
        )
        return (scores, dprobs)

    statistic_shape = (KEY_VALUE_HEADS, 2, present_rows)
    stats = (
        jnp.full(statistic_shape, -1e30, jnp.float32),
        jnp.zeros(statistic_shape, jnp.float32),
        jnp.zeros(statistic_shape, jnp.float32),
    )
    allowed_list = []
    for block_opening, block_extent in block_list:
        tile_pos = key_pos[block_opening : block_opening + block_extent]
        tile_ok = key_ok[block_opening : block_opening + block_extent]
        tile_idx = key_idx[block_opening : block_opening + block_extent]
        allowed = (
            tile_ok[None, :]
            & (tile_idx[None, :] <= query_idx[:, None])
            & (query_pos[:, None] - tile_pos[None, :] < WINDOW)
        )
        allowed_list.append(allowed)
        first_running_max, first_running_sum, first_running_dot = stats
        first_scores, first_dprobs = block_scores(block_opening, block_extent)
        live_scores = jnp.where(allowed, first_scores, -jnp.inf)
        new_max = jnp.maximum(first_running_max, jnp.max(live_scores, axis=-1))
        rescale = jnp.exp(first_running_max - new_max)
        weights = jnp.exp(live_scores - new_max[..., None])
        stats = (
            new_max,
            first_running_sum * rescale + jnp.sum(weights, axis=-1),
            first_running_dot * rescale + jnp.sum(weights * first_dprobs, axis=-1),
        )
    running_max, running_sum, running_dot = stats
    log_total = running_max + jnp.log(running_sum)
    row_delta = running_dot / running_sum
    query_accumulator = jnp.zeros((present_rows, KEY_VALUE_HEADS, 2, HEAD_SIZE), jnp.float32)
    key_blocks = []
    value_blocks = []
    for block_number in range(len(block_list)):
        block_opening, block_extent = block_list[block_number]
        allowed = allowed_list[block_number]
        second_key_piece = key_complete[block_opening : block_opening + block_extent].reshape(
            block_extent, KEY_VALUE_HEADS, HEAD_SIZE
        )
        second_scores, second_dprobs = block_scores(block_opening, block_extent)
        second_weights = jnp.where(allowed, jnp.exp(second_scores - log_total[..., None]), 0.0)
        half_weights = second_weights.astype(jnp.bfloat16)
        dscores = (second_weights * (second_dprobs - row_delta[..., None])).astype(jnp.bfloat16)
        query_part = jnp.einsum(
            "gjtk,kgd->tgjd", dscores, second_key_piece, preferred_element_type=jnp.float32
        )
        key_part = (
            jnp.einsum(
                "gjtk,tgjd->kgd", dscores, query_quad_rows, preferred_element_type=jnp.float32
            )
            * SCORE_SCALE
        ).astype(jnp.bfloat16)
        value_part = jnp.einsum(
            "gjtk,tgjd->kgd", half_weights, masked_quad_scores, preferred_element_type=jnp.float32
        ).astype(jnp.bfloat16)
        query_part, key_part, value_part = (
            query_part,
            key_part.reshape(block_extent, feature_columns),
            value_part.reshape(block_extent, feature_columns),
        )
        query_accumulator = query_accumulator + query_part
        key_blocks.append(key_part)
        value_blocks.append(value_part)
    key_terms = jnp.concatenate(key_blocks, axis=0).reshape(
        REACH + 1, present_rows, feature_columns
    )
    value_terms = jnp.concatenate(value_blocks, axis=0).reshape(
        REACH + 1, present_rows, feature_columns
    )
    key_sum = key_terms[REACH].astype(jnp.float32)
    value_sum = value_terms[REACH].astype(jnp.float32)
    for distance in range(1, REACH + 1):
        back_keys, back_values = shifted(
            (key_terms[REACH - distance], value_terms[REACH - distance]), "context", -distance
        )
        key_sum = key_sum + back_keys.astype(jnp.float32)
        value_sum = value_sum + back_values.astype(jnp.float32)
    grad_keys = key_sum.astype(jnp.bfloat16)
    value_gradient = value_sum.astype(jnp.bfloat16)
    grad_queries = (
        (query_accumulator * SCORE_SCALE)
        .astype(jnp.bfloat16)
        .reshape(1, present_rows, HQ * HEAD_SIZE)
    )
    adapter_term = ADAPTER_SCALE * jnp.einsum(
        "ud,ug->dg", adapter_hidden[0], value_gradient, preferred_element_type=jnp.float32
    )
    adapter_whole = lax.psum(adapter_term, "context")
    adapter_grad = lax.psum_scatter(adapter_whole, "fsdp", scatter_dimension=1, tiled=True)
    return (grad_queries, grad_keys[None], value_gradient[None], adapter_grad)


MESH = pl.DeviceIdType.MESH
T = 128
D = HEAD_SIZE
EXP2_SCALE = SCORE_SCALE * math.log2(math.e)


def lower_shard(block):
    return max(0, 2 * block - REACH)


def cols(index):
    return pl.ds(pl.multiple_of(index * D, D), D)


def head_kernel(
    shards, count_ref, offset_ref, hidden_ref, k_ref, v_ref, q_ref, do_ref,
    dq_out, dk_out, dv_out, ad_out,
    side, sbuf, hbuf, kbuf, vbuf, qbuf, dobuf, ktbuf, pbuf, acc, rx, fin, dqbuf, adpart, adbuf,
    s_send, s_recv, h_send, h_recv, k_send, k_recv, v_send, v_recv, q_send, q_recv, do_send, do_recv,
    fk_send, fv_send, x_send, x_recv, dq_send, dq_recv, kv_send, kv_recv, ad_send, ad_recv,
):
    me = lax.axis_index("context")
    core = lax.axis_index("fsdp")
    other = 1 - core
    row = me // KEY_VALUE_HEADS
    head = me % KEY_VALUE_HEADS
    blocks = shards // 2

    def is_self(chip, dev):
        return jnp.logical_and(chip == me, dev == core)

    def remote(src, dst, ssem, rsem, chip, dev):
        return pltpu.make_async_remote_copy(
            src_ref=src, dst_ref=dst, send_sem=ssem, recv_sem=rsem,
            device_id={"context": chip, "fsdp": dev}, device_id_type=MESH,
        )

    def send(src, dst, ssem, rsem, chip, dev):
        mine = is_self(chip, dev)

        @pl.when(mine)
        def _():
            pltpu.make_async_copy(src, dst, rsem).start()

        @pl.when(jnp.logical_not(mine))
        def _():
            remote(src, dst, ssem, rsem, chip, dev).start()

    def sent(src, dst, ssem, rsem, chip, dev):
        @pl.when(jnp.logical_not(is_self(chip, dev)))
        def _():
            remote(src, dst, ssem, rsem, chip, dev).wait_send()

    def arrived(dst, rsem):
        pltpu.make_async_copy(dst, dst, rsem).wait()

    barrier = pltpu.get_barrier_semaphore()

    def greet(step, carry):
        chip = lax.rem(me + step, shards)

        @pl.when(step > 0)
        def _():
            pl.semaphore_signal(
                barrier, inc=1, device_id={"context": chip, "fsdp": core}, device_id_type=MESH
            )

        pl.semaphore_signal(
            barrier, inc=1, device_id={"context": chip, "fsdp": other}, device_id_type=MESH
        )
        return carry

    lax.fori_loop(0, shards, greet, 0)
    side[0:1, :] = jnp.full((1, T), count_ref[0, 0].astype(jnp.float32))
    side[1:2, :] = jnp.full((1, T), offset_ref[0, 0].astype(jnp.float32))
    acc[...] = jnp.zeros_like(acc)
    adpart[...] = jnp.zeros_like(adpart)
    pl.semaphore_wait(barrier, 2 * shards - 1)

    def target(step):
        kv_head = jnp.bitwise_xor(step, head)
        return kv_head, core * KEY_VALUE_HEADS + kv_head

    def side_args(step, dev):
        kv_head, chip = target(step)
        return side, sbuf.at[me], s_send.at[kv_head, dev], s_recv.at[me], chip, dev

    def hidden_args(step):
        kv_head, chip = target(step)
        return hidden_ref, hbuf.at[me], h_send.at[kv_head], h_recv.at[me], chip, 1

    def k_args(step):
        kv_head, chip = target(step)
        return k_ref.at[:, cols(kv_head)], kbuf.at[me], k_send.at[kv_head], k_recv.at[me], chip, me % 2

    def v_args(step):
        kv_head, chip = target(step)
        return v_ref.at[:, cols(kv_head)], vbuf.at[me], v_send.at[kv_head], v_recv.at[me], chip, me % 2

    def q_args(step, dev):
        kv_head, chip = target(step)
        return (q_ref.at[:, cols(2 * kv_head + dev)], qbuf.at[me], q_send.at[kv_head, dev],
                q_recv.at[me], chip, dev)

    def do_args(step, dev):
        kv_head, chip = target(step)
        return (do_ref.at[:, cols(2 * kv_head + dev)], dobuf.at[me], do_send.at[kv_head, dev],
                do_recv.at[me], chip, dev)

    def loop(count, body):
        def step_fn(step, carry):
            body(step)
            return carry
        lax.fori_loop(0, count, step_fn, 0)

    def first(act):
        def body(step):
            act(*k_args(step))
            act(*v_args(step))
            act(*side_args(step, 0))
            act(*side_args(step, 1))
        return body

    def second(act):
        def body(step):
            act(*q_args(step, 0))
            act(*q_args(step, 1))
        return body

    def third(act):
        def body(step):
            act(*do_args(step, 0))
            act(*do_args(step, 1))
            act(*hidden_args(step))
        return body

    loop(KEY_VALUE_HEADS, first(send))
    loop(KEY_VALUE_HEADS, second(send))
    loop(KEY_VALUE_HEADS, third(send))

    def forward(step):
        shard = 2 * step + core
        arrived(kbuf.at[shard], k_recv.at[shard])
        remote(kbuf.at[shard], kbuf.at[shard], fk_send.at[shard], k_recv.at[shard], me, other).start()
        arrived(vbuf.at[shard], v_recv.at[shard])
        remote(vbuf.at[shard], vbuf.at[shard], fv_send.at[shard], v_recv.at[shard], me, other).start()

    loop(blocks, forward)

    def from_sibling(step):
        shard = 2 * step + other
        arrived(kbuf.at[shard], k_recv.at[shard])
        arrived(vbuf.at[shard], v_recv.at[shard])

    loop(blocks, from_sibling)

    def side_in(step):
        arrived(sbuf.at[step], s_recv.at[step])

    loop(shards, side_in)

    slot = lax.broadcasted_iota(jnp.int32, (T, 2 * T), 0).astype(jnp.float32)
    lane = lax.broadcasted_iota(jnp.int32, (1, T), 1).astype(jnp.float32)
    starts = []
    total = 0
    for block in range(blocks):
        starts.append(total)
        total += (2 * block + 2 - lower_shard(block)) * T

    def dot(a, b, dims):
        return lax.dot_general(a, b, (dims, ((), ())), preferred_element_type=jnp.float32)

    for shard in range(shards):
        ktbuf[:, shard * T : (shard + 1) * T] = kbuf[shard].T

    for block in range(blocks):
        low, high = lower_shard(block), 2 * block + 2
        span = (high - low) * T
        arrived(qbuf.at[2 * block], q_recv.at[2 * block])
        arrived(qbuf.at[2 * block + 1], q_recv.at[2 * block + 1])
        q = qbuf[2 * block : 2 * block + 2].reshape(2 * T, D)
        k = kbuf[low:high].reshape(span, D)
        raw = dot(k, q, ((1,), (1,)))
        q_pos = jnp.concatenate(
            [sbuf[2 * block, 1:2, :] + lane, sbuf[2 * block + 1, 1:2, :] + lane], axis=1
        )
        q_index = jnp.concatenate([lane, lane + T], axis=1)
        pieces = []
        for shard in range(low, high):
            count = sbuf[shard, 0:1, :]
            top = jnp.concatenate([count, count], axis=1) - 1.0
            if shard >= 2 * block:
                top = jnp.minimum(top, q_index - (shard - 2 * block) * T)
            allowed = slot <= top
            if (high - shard) * T > WINDOW:
                offset = sbuf[shard, 1:2, :]
                bottom = q_pos - jnp.concatenate([offset, offset], axis=1) - WINDOW
                allowed = jnp.logical_and(allowed, slot > bottom)
            piece = raw[(shard - low) * T : (shard - low + 1) * T] * EXP2_SCALE
            pieces.append(jnp.where(allowed, piece, -1e30))
        peak = pieces[0].max(axis=0, keepdims=True)
        for piece in pieces[1:]:
            peak = jnp.maximum(peak, piece.max(axis=0, keepdims=True))
        weights = [jnp.exp2(piece - peak) for piece in pieces]
        norm = weights[0].sum(axis=0, keepdims=True)
        for weight in weights[1:]:
            norm = norm + weight.sum(axis=0, keepdims=True)
        inverse = 1.0 / norm
        for number, weight in enumerate(weights):
            begin = starts[block] + number * T
            pbuf[begin : begin + T, :] = weight * inverse

    def swap_args(block):
        return (acc.at[other, pl.ds(2 * T * block, 2 * T)], rx.at[block], x_send.at[block],
                x_recv.at[block], me, other)

    def dq_args(shard):
        return (dqbuf.at[shard], dq_out.at[:, cols(2 * head + core)], dq_send.at[shard],
                dq_recv.at[2 * head + core], shard, row)

    def kv_args(shard, out, kind):
        return (fin.at[shard], out.at[:, cols(head)], kv_send.at[shard],
                kv_recv.at[kind, head], shard, row)

    def kv_each(shard, act):
        @pl.when(core == 0)
        def _():
            act(*kv_args(shard, dk_out, 0))

        @pl.when(core == 1)
        def _():
            act(*kv_args(shard, dv_out, 1))

    factor = jnp.where(core == 0, SCORE_SCALE, 1.0).astype(jnp.float32)

    def turned(base, step):
        return base + jnp.bitwise_xor(step, lax.rem(me, 4))

    def finish(pair):
        for block in (2 * pair, 2 * pair + 1):
            arrived(rx.at[block], x_recv.at[block])
            whole = acc[core, pl.ds(2 * T * block, 2 * T), :] + rx[block]
            half = (whole * factor).astype(jnp.bfloat16)
            fin[2 * block] = half[:T]
            fin[2 * block + 1] = half[T:]
        loop(4, lambda step: kv_each(turned(4 * pair, step), send))

    def swap(pair):
        remote(*swap_args(2 * pair)).start()
        remote(*swap_args(2 * pair + 1)).start()

    def block_grads(block):
        low, high = lower_shard(block), 2 * block + 2
        span = (high - low) * T
        grads = []
        for shard in (2 * block, 2 * block + 1):
            arrived(dobuf.at[shard], do_recv.at[shard])
            count = sbuf[shard, 0:1, :]
            grads.append(jnp.where(slot[:, :D] < count, dobuf[shard].astype(jnp.float32), 0.0))
        grad = jnp.concatenate(grads, axis=0).astype(jnp.bfloat16)
        q = qbuf[2 * block : 2 * block + 2].reshape(2 * T, D)
        v = vbuf[low:high].reshape(span, D)
        probs = pbuf[starts[block] : starts[block] + span, :]
        dprobs = dot(v, grad, ((1,), (1,)))
        delta = jnp.sum(probs * dprobs, axis=0, keepdims=True)
        dscores = (probs * (dprobs - delta)).astype(jnp.bfloat16)
        dq = dot(ktbuf[:, low * T : high * T], dscores, ((1,), (0,))).T * SCORE_SCALE
        dqbuf[2 * block] = dq[:T].astype(jnp.bfloat16)
        dqbuf[2 * block + 1] = dq[T:].astype(jnp.bfloat16)
        acc[0, low * T : high * T, :] += dot(dscores, q, ((1,), (0,)))
        acc[1, low * T : high * T, :] += dot(probs.astype(jnp.bfloat16), grad, ((1,), (0,)))

    pairs = blocks // 2

    def pair_grads(pair, order):
        for block in order:
            block_grads(2 * pair + block)
        loop(4, lambda step: send(*dq_args(turned(4 * pair, step))))

    @pl.when(row == 0)
    def _():
        for pair in reversed(range(pairs)):
            pair_grads(pair, (1, 0))
            swap(pair)
            if pair + 1 < pairs:
                finish(pair + 1)
        finish(0)

    @pl.when(row == 1)
    def _():
        for pair in range(pairs):
            pair_grads(pair, (0, 1))
        for pair in range(pairs):
            swap(pair)
        for pair in range(pairs):
            finish(pair)

    half_heads = KEY_VALUE_HEADS // 2

    def ad_args(step):
        chip = lax.rem(me + step, shards)
        return (adpart, adbuf.at[row, :, cols(head % half_heads)], ad_send.at[step],
                ad_recv.at[row, head % half_heads], chip, head // half_heads)

    @pl.when(core == 1)
    def _():
        for shard in range(shards):
            arrived(hbuf.at[shard], h_recv.at[shard])
            adpart[...] += dot(hbuf[shard], fin[shard], ((1,), (0,)))
        adpart[...] *= ADAPTER_SCALE
        loop(shards, lambda step: send(*ad_args(step)))

    loop(KEY_VALUE_HEADS, first(sent))
    loop(KEY_VALUE_HEADS, second(sent))
    loop(KEY_VALUE_HEADS, third(sent))

    def forward_sent(step):
        shard = 2 * step + core
        remote(kbuf.at[shard], kbuf.at[shard], fk_send.at[shard], k_recv.at[shard], me, other).wait_send()
        remote(vbuf.at[shard], vbuf.at[shard], fv_send.at[shard], v_recv.at[shard], me, other).wait_send()

    loop(blocks, forward_sent)
    for block in range(blocks):
        remote(*swap_args(block)).wait_send()
    loop(shards, lambda shard: sent(*dq_args(shard)))
    loop(shards, lambda shard: kv_each(shard, sent))

    @pl.when(core == 1)
    def _():
        loop(shards, lambda step: sent(*ad_args(step)))

    loop(HQ, lambda index: arrived(dq_out.at[:, cols(index)], dq_recv.at[index]))
    loop(KEY_VALUE_HEADS, lambda index: arrived(dk_out.at[:, cols(index)], kv_recv.at[0, index]))
    loop(KEY_VALUE_HEADS, lambda index: arrived(dv_out.at[:, cols(index)], kv_recv.at[1, index]))
    for source in range(2):
        for index in range(half_heads):
            arrived(adbuf.at[source, :, index * D : (index + 1) * D], ad_recv.at[source, index])
    ad_out[...] = adbuf[0] + adbuf[1]


def by_head(shards, queries, keys, values, output_gradient, adapter_hidden, counts, offsets):
    blocks = shards // 2
    total = sum((2 * block + 2 - lower_shard(block)) * T for block in range(blocks))
    bf16, f32 = jnp.bfloat16, jnp.float32
    dma = pltpu.SemaphoreType.DMA
    anywhere = pl.BlockSpec(memory_space=pl.ANY)
    vmem = pl.BlockSpec(memory_space=pltpu.VMEM)
    scalar = pl.BlockSpec(memory_space=pltpu.SMEM)
    dq, dk, dv, adapter = pl.pallas_call(
        functools.partial(head_kernel, shards),
        out_shape=(
            jax.ShapeDtypeStruct((T, HQ * D), bf16),
            jax.ShapeDtypeStruct((T, KEY_VALUE_HEADS * D), bf16),
            jax.ShapeDtypeStruct((T, KEY_VALUE_HEADS * D), bf16),
            jax.ShapeDtypeStruct((ADAPTER_RANK, KEY_VALUE_HEADS * D // 2), f32),
        ),
        in_specs=[scalar] * 2 + [anywhere] * 5,
        out_specs=(anywhere, anywhere, anywhere, vmem),
        scratch_shapes=[
            pltpu.VMEM((2, T), f32),
            pltpu.VMEM((shards, 2, T), f32),
            pltpu.VMEM((shards, ADAPTER_RANK, T), bf16),
            pltpu.VMEM((shards, T, D), bf16),
            pltpu.VMEM((shards, T, D), bf16),
            pltpu.VMEM((shards, T, D), bf16),
            pltpu.VMEM((shards, T, D), bf16),
            pltpu.VMEM((D, shards * T), bf16),
            pltpu.VMEM((total, 2 * T), f32),
            pltpu.VMEM((2, shards * T, D), f32),
            pltpu.VMEM((blocks, 2 * T, D), f32),
            pltpu.VMEM((shards, T, D), bf16),
            pltpu.VMEM((shards, T, D), bf16),
            pltpu.VMEM((ADAPTER_RANK, D), f32),
            pltpu.VMEM((2, ADAPTER_RANK, KEY_VALUE_HEADS * D // 2), f32),
            dma((KEY_VALUE_HEADS, 2)), dma((shards,)),
            dma((KEY_VALUE_HEADS,)), dma((shards,)),
            dma((KEY_VALUE_HEADS,)), dma((shards,)),
            dma((KEY_VALUE_HEADS,)), dma((shards,)),
            dma((KEY_VALUE_HEADS, 2)), dma((shards,)),
            dma((KEY_VALUE_HEADS, 2)), dma((shards,)),
            dma((shards,)), dma((shards,)),
            dma((blocks,)), dma((blocks,)),
            dma((shards,)), dma((HQ,)),
            dma((shards,)), dma((2, KEY_VALUE_HEADS)),
            dma((shards,)), dma((2, KEY_VALUE_HEADS // 2)),
        ],
        compiler_params=pltpu.CompilerParams(
            collective_id=0, has_side_effects=True, vmem_limit_bytes=63 * 1024 * 1024
        ),
    )(counts, offsets, adapter_hidden[0].T, keys[0], values[0], queries[0], output_gradient[0])
    return dq[None], dk[None], dv[None], adapter


def solution(mesh):
    shards = mesh.shape["context"]
    fits = shards == 2 * KEY_VALUE_HEADS and mesh.shape["fsdp"] == 2
    body = functools.partial(by_head, shards) if fits else local
    in_specs = (
        P("fsdp", "context", None),
        P("fsdp", "context", None),
        P("fsdp", "context", None),
        P("fsdp", "context", None),
        P("fsdp", "context", None),
        P("fsdp", "context"),
        P("fsdp", "context"),
    )
    out_specs = (
        P("fsdp", "context", None),
        P("fsdp", "context", None),
        P("fsdp", "context", None),
        P(None, "fsdp"),
    )
    return jax.shard_map(body, mesh=mesh, in_specs=in_specs, out_specs=out_specs, check_vma=False)
```

```python
import functools
import math

import jax
import jax.numpy as jnp
from jax import lax
from jax.experimental import pallas as pl
from jax.experimental.pallas import tpu as pltpu
from jax.sharding import PartitionSpec as P

HQ = 16
KEY_VALUE_HEADS = 8
HEAD_SIZE = 128
WINDOW = 1024
REACH = 10
ADAPTER_RANK = 16


SCORE_SCALE = 168.0 ** (-0.5)
ADAPTER_SCALE = 2.0


def shifted(value, axis, steps):
    count = lax.axis_size(axis)
    initial, last = (max(0, -steps), min(count, count - steps))
    return lax.ppermute(value, axis, [(source, source + steps) for source in range(initial, last)])


def local(queries, keys, values, output_gradient, adapter_hidden, counts, offsets):
    present_rows = queries.shape[1]
    feature_columns = keys.shape[2]
    slot_ids = jnp.arange(present_rows, dtype=jnp.int32)
    own_offset = offsets[0, 0]
    own_count = counts[0, 0]
    valid_rows = slot_ids < own_count
    masked_scores = jnp.where(
        valid_rows[:, None], output_gradient[0], jnp.zeros_like(output_gradient[0])
    )
    query_quad_rows = queries[0].reshape(present_rows, KEY_VALUE_HEADS, 2, HEAD_SIZE)
    masked_quad_scores = masked_scores.reshape(present_rows, KEY_VALUE_HEADS, 2, HEAD_SIZE)
    own_items = (keys[0], values[0], offsets[0], counts[0])
    arrived = []
    current = own_items
    for hop_index in range(REACH):
        current = shifted((current[0], current[1], current[2], current[3]), "context", 1)
        arrived.append(current)
    window_items = arrived[::-1] + [own_items]
    key_complete = jnp.concatenate([shard_data[0] for shard_data in window_items], axis=0)
    value_complete = jnp.concatenate([shard_data[1] for shard_data in window_items], axis=0)
    key_pos = jnp.concatenate([shard_data[2][0] + slot_ids for shard_data in window_items], axis=0)
    key_ok = jnp.concatenate([slot_ids < shard_data[3][0] for shard_data in window_items], axis=0)
    total_keys = key_complete.shape[0]
    key_idx = jnp.arange(total_keys, dtype=jnp.int32)
    query_idx = REACH * present_rows + slot_ids
    query_pos = own_offset + slot_ids
    block_cap = 512
    block_list = []
    block_begin = 0
    while block_begin < total_keys:
        block_extent = min(block_cap, total_keys - block_begin)
        block_list.append((block_begin, block_extent))
        block_begin = block_begin + block_extent

    def block_scores(block_opening, block_extent):
        key_piece = key_complete[block_opening : block_opening + block_extent].reshape(
            block_extent, KEY_VALUE_HEADS, HEAD_SIZE
        )
        value_piece = value_complete[block_opening : block_opening + block_extent].reshape(
            block_extent, KEY_VALUE_HEADS, HEAD_SIZE
        )
        scores = (
            jnp.einsum(
                "tgjd,kgd->gjtk", query_quad_rows, key_piece, preferred_element_type=jnp.float32
            )
            * SCORE_SCALE
        )
        dprobs = jnp.einsum(
            "tgjd,kgd->gjtk", masked_quad_scores, value_piece, preferred_element_type=jnp.float32
        )
        return (scores, dprobs)

    statistic_shape = (KEY_VALUE_HEADS, 2, present_rows)
    stats = (
        jnp.full(statistic_shape, -1e30, jnp.float32),
        jnp.zeros(statistic_shape, jnp.float32),
        jnp.zeros(statistic_shape, jnp.float32),
    )
    allowed_list = []
    for block_opening, block_extent in block_list:
        tile_pos = key_pos[block_opening : block_opening + block_extent]
        tile_ok = key_ok[block_opening : block_opening + block_extent]
        tile_idx = key_idx[block_opening : block_opening + block_extent]
        allowed = (
            tile_ok[None, :]
            & (tile_idx[None, :] <= query_idx[:, None])
            & (query_pos[:, None] - tile_pos[None, :] < WINDOW)
        )
        allowed_list.append(allowed)
        first_running_max, first_running_sum, first_running_dot = stats
        first_scores, first_dprobs = block_scores(block_opening, block_extent)
        live_scores = jnp.where(allowed, first_scores, -jnp.inf)
        new_max = jnp.maximum(first_running_max, jnp.max(live_scores, axis=-1))
        rescale = jnp.exp(first_running_max - new_max)
        weights = jnp.exp(live_scores - new_max[..., None])
        stats = (
            new_max,
            first_running_sum * rescale + jnp.sum(weights, axis=-1),
            first_running_dot * rescale + jnp.sum(weights * first_dprobs, axis=-1),
        )
    running_max, running_sum, running_dot = stats
    log_total = running_max + jnp.log(running_sum)
    row_delta = running_dot / running_sum
    query_accumulator = jnp.zeros((present_rows, KEY_VALUE_HEADS, 2, HEAD_SIZE), jnp.float32)
    key_blocks = []
    value_blocks = []
    for block_number in range(len(block_list)):
        block_opening, block_extent = block_list[block_number]
        allowed = allowed_list[block_number]
        second_key_piece = key_complete[block_opening : block_opening + block_extent].reshape(
            block_extent, KEY_VALUE_HEADS, HEAD_SIZE
        )
        second_scores, second_dprobs = block_scores(block_opening, block_extent)
        second_weights = jnp.where(allowed, jnp.exp(second_scores - log_total[..., None]), 0.0)
        half_weights = second_weights.astype(jnp.bfloat16)
        dscores = (second_weights * (second_dprobs - row_delta[..., None])).astype(jnp.bfloat16)
        query_part = jnp.einsum(
            "gjtk,kgd->tgjd", dscores, second_key_piece, preferred_element_type=jnp.float32
        )
        key_part = (
            jnp.einsum(
                "gjtk,tgjd->kgd", dscores, query_quad_rows, preferred_element_type=jnp.float32
            )
            * SCORE_SCALE
        ).astype(jnp.bfloat16)
        value_part = jnp.einsum(
            "gjtk,tgjd->kgd", half_weights, masked_quad_scores, preferred_element_type=jnp.float32
        ).astype(jnp.bfloat16)
        query_part, key_part, value_part = (
            query_part,
            key_part.reshape(block_extent, feature_columns),
            value_part.reshape(block_extent, feature_columns),
        )
        query_accumulator = query_accumulator + query_part
        key_blocks.append(key_part)
        value_blocks.append(value_part)
    key_terms = jnp.concatenate(key_blocks, axis=0).reshape(
        REACH + 1, present_rows, feature_columns
    )
    value_terms = jnp.concatenate(value_blocks, axis=0).reshape(
        REACH + 1, present_rows, feature_columns
    )
    key_sum = key_terms[REACH].astype(jnp.float32)
    value_sum = value_terms[REACH].astype(jnp.float32)
    for distance in range(1, REACH + 1):
        back_keys, back_values = shifted(
            (key_terms[REACH - distance], value_terms[REACH - distance]), "context", -distance
        )
        key_sum = key_sum + back_keys.astype(jnp.float32)
        value_sum = value_sum + back_values.astype(jnp.float32)
    grad_keys = key_sum.astype(jnp.bfloat16)
    value_gradient = value_sum.astype(jnp.bfloat16)
    grad_queries = (
        (query_accumulator * SCORE_SCALE)
        .astype(jnp.bfloat16)
        .reshape(1, present_rows, HQ * HEAD_SIZE)
    )
    adapter_term = ADAPTER_SCALE * jnp.einsum(
        "ud,ug->dg", adapter_hidden[0], value_gradient, preferred_element_type=jnp.float32
    )
    adapter_whole = lax.psum(adapter_term, "context")
    adapter_grad = lax.psum_scatter(adapter_whole, "fsdp", scatter_dimension=1, tiled=True)
    return (grad_queries, grad_keys[None], value_gradient[None], adapter_grad)


MESH = pl.DeviceIdType.MESH
T = 128
D = HEAD_SIZE
EXP2_SCALE = SCORE_SCALE * math.log2(math.e)


def lower_shard(block):
    return max(0, 2 * block - REACH)


def cols(index):
    return pl.ds(pl.multiple_of(index * D, D), D)


def head_kernel(
    shards, count_ref, offset_ref, hidden_ref, k_ref, v_ref, q_ref, do_ref,
    dq_out, dk_out, dv_out, adbuf,
    side, sbuf, hbuf, kbuf, vbuf, qbuf, dobuf, ktbuf, pbuf, acc, rx, fin, dqbuf, adpart,
    s_send, s_recv, h_send, h_recv, k_send, k_recv, v_send, v_recv, q_send, q_recv, do_send, do_recv,
    fk_send, fv_send, x_send, x_recv, dq_send, dq_recv, kv_send, kv_recv, ad_send, ad_recv,
):
    me = lax.axis_index("context")
    core = lax.axis_index("fsdp")
    other = 1 - core
    row = me // KEY_VALUE_HEADS
    head = me % KEY_VALUE_HEADS
    blocks = shards // 2

    def is_self(chip, dev):
        return jnp.logical_and(chip == me, dev == core)

    def remote(src, dst, ssem, rsem, chip, dev):
        return pltpu.make_async_remote_copy(
            src_ref=src, dst_ref=dst, send_sem=ssem, recv_sem=rsem,
            device_id={"context": chip, "fsdp": dev}, device_id_type=MESH,
        )

    def send(src, dst, ssem, rsem, chip, dev):
        mine = is_self(chip, dev)

        @pl.when(mine)
        def _():
            pltpu.make_async_copy(src, dst, rsem).start()

        @pl.when(jnp.logical_not(mine))
        def _():
            remote(src, dst, ssem, rsem, chip, dev).start()

    def sent(src, dst, ssem, rsem, chip, dev):
        @pl.when(jnp.logical_not(is_self(chip, dev)))
        def _():
            remote(src, dst, ssem, rsem, chip, dev).wait_send()

    def arrived(dst, rsem):
        pltpu.make_async_copy(dst, dst, rsem).wait()

    barrier = pltpu.get_barrier_semaphore()

    def greet(step, carry):
        chip = lax.rem(me + step, shards)

        @pl.when(step > 0)
        def _():
            pl.semaphore_signal(
                barrier, inc=1, device_id={"context": chip, "fsdp": core}, device_id_type=MESH
            )

        pl.semaphore_signal(
            barrier, inc=1, device_id={"context": chip, "fsdp": other}, device_id_type=MESH
        )
        return carry

    lax.fori_loop(0, shards, greet, 0)
    side[0:1, :] = jnp.full((1, T), count_ref[0, 0].astype(jnp.float32))
    side[1:2, :] = jnp.full((1, T), offset_ref[0, 0].astype(jnp.float32))
    acc[...] = jnp.zeros_like(acc)
    adpart[...] = jnp.zeros_like(adpart)
    pl.semaphore_wait(barrier, 2 * shards - 1)

    def target(step):
        kv_head = jnp.bitwise_xor(step, head)
        return kv_head, core * KEY_VALUE_HEADS + kv_head

    def side_args(step, dev):
        kv_head, chip = target(step)
        return side, sbuf.at[me], s_send.at[kv_head, dev], s_recv.at[me], chip, dev

    def hidden_args(step):
        kv_head, chip = target(step)
        return hidden_ref, hbuf.at[me], h_send.at[kv_head], h_recv.at[me], chip, 1

    def k_args(step):
        kv_head, chip = target(step)
        return k_ref.at[:, cols(kv_head)], kbuf.at[me], k_send.at[kv_head], k_recv.at[me], chip, me % 2

    def v_args(step):
        kv_head, chip = target(step)
        return v_ref.at[:, cols(kv_head)], vbuf.at[me], v_send.at[kv_head], v_recv.at[me], chip, me % 2

    def q_args(step, dev):
        kv_head, chip = target(step)
        return (q_ref.at[:, cols(2 * kv_head + dev)], qbuf.at[me], q_send.at[kv_head, dev],
                q_recv.at[me], chip, dev)

    def do_args(step, dev):
        kv_head, chip = target(step)
        return (do_ref.at[:, cols(2 * kv_head + dev)], dobuf.at[me], do_send.at[kv_head, dev],
                do_recv.at[me], chip, dev)

    def loop(count, body):
        def step_fn(step, carry):
            body(step)
            return carry
        lax.fori_loop(0, count, step_fn, 0)

    def first(act):
        def body(step):
            act(*k_args(step))
            act(*v_args(step))
            act(*side_args(step, 0))
            act(*side_args(step, 1))
        return body

    def second(act):
        def body(step):
            act(*q_args(step, 0))
            act(*q_args(step, 1))
        return body

    def third(act):
        def body(step):
            act(*do_args(step, 0))
            act(*do_args(step, 1))
            act(*hidden_args(step))
        return body

    loop(KEY_VALUE_HEADS, first(send))
    loop(KEY_VALUE_HEADS, second(send))
    loop(KEY_VALUE_HEADS, third(send))

    def forward(step):
        shard = 2 * step + core
        arrived(kbuf.at[shard], k_recv.at[shard])
        remote(kbuf.at[shard], kbuf.at[shard], fk_send.at[shard], k_recv.at[shard], me, other).start()
        arrived(vbuf.at[shard], v_recv.at[shard])
        remote(vbuf.at[shard], vbuf.at[shard], fv_send.at[shard], v_recv.at[shard], me, other).start()

    loop(blocks, forward)

    def from_sibling(step):
        shard = 2 * step + other
        arrived(kbuf.at[shard], k_recv.at[shard])
        arrived(vbuf.at[shard], v_recv.at[shard])

    loop(blocks, from_sibling)

    def side_in(step):
        arrived(sbuf.at[step], s_recv.at[step])

    loop(shards, side_in)

    slot = lax.broadcasted_iota(jnp.int32, (T, 2 * T), 0).astype(jnp.float32)
    lane = lax.broadcasted_iota(jnp.int32, (1, T), 1).astype(jnp.float32)
    starts = []
    total = 0
    for block in range(blocks):
        starts.append(total)
        total += (2 * block + 2 - lower_shard(block)) * T

    def dot(a, b, dims):
        return lax.dot_general(a, b, (dims, ((), ())), preferred_element_type=jnp.float32)

    for shard in range(shards):
        ktbuf[:, shard * T : (shard + 1) * T] = kbuf[shard].T

    for block in range(blocks):
        low, high = lower_shard(block), 2 * block + 2
        span = (high - low) * T
        arrived(qbuf.at[2 * block], q_recv.at[2 * block])
        arrived(qbuf.at[2 * block + 1], q_recv.at[2 * block + 1])
        q = qbuf[2 * block : 2 * block + 2].reshape(2 * T, D)
        k = kbuf[low:high].reshape(span, D)
        raw = dot(k, q, ((1,), (1,)))
        q_pos = jnp.concatenate(
            [sbuf[2 * block, 1:2, :] + lane, sbuf[2 * block + 1, 1:2, :] + lane], axis=1
        )
        q_index = jnp.concatenate([lane, lane + T], axis=1)
        pieces = []
        for shard in range(low, high):
            count = sbuf[shard, 0:1, :]
            top = jnp.concatenate([count, count], axis=1) - 1.0
            if shard >= 2 * block:
                top = jnp.minimum(top, q_index - (shard - 2 * block) * T)
            allowed = slot <= top
            if (high - shard) * T > WINDOW:
                offset = sbuf[shard, 1:2, :]
                bottom = q_pos - jnp.concatenate([offset, offset], axis=1) - WINDOW
                allowed = jnp.logical_and(allowed, slot > bottom)
            piece = raw[(shard - low) * T : (shard - low + 1) * T] * EXP2_SCALE
            pieces.append(jnp.where(allowed, piece, -1e30))
        peak = pieces[0].max(axis=0, keepdims=True)
        for piece in pieces[1:]:
            peak = jnp.maximum(peak, piece.max(axis=0, keepdims=True))
        weights = [jnp.exp2(piece - peak) for piece in pieces]
        norm = weights[0].sum(axis=0, keepdims=True)
        for weight in weights[1:]:
            norm = norm + weight.sum(axis=0, keepdims=True)
        inverse = 1.0 / norm
        for number, weight in enumerate(weights):
            begin = starts[block] + number * T
            pbuf[begin : begin + T, :] = weight * inverse

    def swap_args(block):
        return (acc.at[other, pl.ds(2 * T * block, 2 * T)], rx.at[block], x_send.at[block],
                x_recv.at[block], me, other)

    def dq_args(shard):
        return (dqbuf.at[shard], dq_out.at[:, cols(2 * head + core)], dq_send.at[shard],
                dq_recv.at[2 * head + core], shard, row)

    def kv_args(shard, out, kind):
        return (fin.at[shard], out.at[:, cols(head)], kv_send.at[shard],
                kv_recv.at[kind, head], shard, row)

    def kv_each(shard, act):
        @pl.when(core == 0)
        def _():
            act(*kv_args(shard, dk_out, 0))

        @pl.when(core == 1)
        def _():
            act(*kv_args(shard, dv_out, 1))

    factor = jnp.where(core == 0, SCORE_SCALE, 1.0).astype(jnp.float32)

    def turned(base, step):
        return base + jnp.bitwise_xor(step, lax.rem(me, 4))

    def finish(pair):
        for block in (2 * pair, 2 * pair + 1):
            arrived(rx.at[block], x_recv.at[block])
            whole = acc[core, pl.ds(2 * T * block, 2 * T), :] + rx[block]
            half = (whole * factor).astype(jnp.bfloat16)
            fin[2 * block] = half[:T]
            fin[2 * block + 1] = half[T:]
        loop(4, lambda step: kv_each(turned(4 * pair, step), send))

    def swap(pair):
        remote(*swap_args(2 * pair)).start()
        remote(*swap_args(2 * pair + 1)).start()

    def block_grads(block):
        low, high = lower_shard(block), 2 * block + 2
        span = (high - low) * T
        grads = []
        for shard in (2 * block, 2 * block + 1):
            arrived(dobuf.at[shard], do_recv.at[shard])
            count = sbuf[shard, 0:1, :]
            grads.append(jnp.where(slot[:, :D] < count, dobuf[shard].astype(jnp.float32), 0.0))
        grad = jnp.concatenate(grads, axis=0).astype(jnp.bfloat16)
        q = qbuf[2 * block : 2 * block + 2].reshape(2 * T, D)
        v = vbuf[low:high].reshape(span, D)
        probs = pbuf[starts[block] : starts[block] + span, :]
        dprobs = dot(v, grad, ((1,), (1,)))
        delta = jnp.sum(probs * dprobs, axis=0, keepdims=True)
        dscores = (probs * (dprobs - delta)).astype(jnp.bfloat16)
        dq = dot(ktbuf[:, low * T : high * T], dscores, ((1,), (0,))).T * SCORE_SCALE
        dqbuf[2 * block] = dq[:T].astype(jnp.bfloat16)
        dqbuf[2 * block + 1] = dq[T:].astype(jnp.bfloat16)
        acc[0, low * T : high * T, :] += dot(dscores, q, ((1,), (0,)))
        acc[1, low * T : high * T, :] += dot(probs.astype(jnp.bfloat16), grad, ((1,), (0,)))

    pairs = blocks // 2

    def pair_grads(pair, order):
        for block in order:
            block_grads(2 * pair + block)
        loop(4, lambda step: send(*dq_args(turned(4 * pair, step))))

    @pl.when(row == 0)
    def _():
        for pair in reversed(range(pairs)):
            pair_grads(pair, (1, 0))
            swap(pair)
            if pair + 1 < pairs:
                finish(pair + 1)
        finish(0)

    @pl.when(row == 1)
    def _():
        for pair in range(pairs):
            pair_grads(pair, (0, 1))
        for pair in range(pairs):
            swap(pair)
        for pair in range(pairs):
            finish(pair)

    half_heads = KEY_VALUE_HEADS // 2

    def ad_args(step):
        chip = lax.rem(me + step, shards)
        return (adpart, adbuf.at[row, :, cols(head % half_heads)], ad_send.at[step],
                ad_recv.at[row, head % half_heads], chip, head // half_heads)

    @pl.when(core == 1)
    def _():
        for shard in range(shards):
            arrived(hbuf.at[shard], h_recv.at[shard])
            adpart[...] += dot(hbuf[shard], fin[shard], ((1,), (0,)))
        adpart[...] *= ADAPTER_SCALE
        loop(shards, lambda step: send(*ad_args(step)))

    loop(KEY_VALUE_HEADS, first(sent))
    loop(KEY_VALUE_HEADS, second(sent))
    loop(KEY_VALUE_HEADS, third(sent))

    def forward_sent(step):
        shard = 2 * step + core
        remote(kbuf.at[shard], kbuf.at[shard], fk_send.at[shard], k_recv.at[shard], me, other).wait_send()
        remote(vbuf.at[shard], vbuf.at[shard], fv_send.at[shard], v_recv.at[shard], me, other).wait_send()

    loop(blocks, forward_sent)
    for block in range(blocks):
        remote(*swap_args(block)).wait_send()
    loop(shards, lambda shard: sent(*dq_args(shard)))
    loop(shards, lambda shard: kv_each(shard, sent))

    @pl.when(core == 1)
    def _():
        loop(shards, lambda step: sent(*ad_args(step)))

    loop(HQ, lambda index: arrived(dq_out.at[:, cols(index)], dq_recv.at[index]))
    loop(KEY_VALUE_HEADS, lambda index: arrived(dk_out.at[:, cols(index)], kv_recv.at[0, index]))
    loop(KEY_VALUE_HEADS, lambda index: arrived(dv_out.at[:, cols(index)], kv_recv.at[1, index]))
    for source in range(2):
        for index in range(half_heads):
            arrived(adbuf.at[source, :, index * D : (index + 1) * D], ad_recv.at[source, index])


def settle_kernel(dq, dk, dv, adapters, dq_out, dk_out, dv_out, ad_out, dq_held, dk_held, dv_held, in_sems, out_sems):
    part = T // 4
    copies = []
    for index, (src, held, dst) in enumerate(
        ((dq, dq_held, dq_out), (dk, dk_held, dk_out), (dv, dv_held, dv_out))
    ):
        for step in range(4):
            rows = pl.ds(step * part, part)
            first = pltpu.make_async_copy(src.at[rows], held.at[rows], in_sems.at[index, step])
            second = pltpu.make_async_copy(held.at[rows], dst.at[0, rows], out_sems.at[index, step])
            first.start()
            copies.append((first, second))
    ad_out[...] = adapters[0] + adapters[1]
    for first, second in copies:
        first.wait()
        second.start()
    for first, second in copies:
        second.wait()


def settle(dq, dk, dv, adapters):
    anywhere = pl.BlockSpec(memory_space=pl.ANY)
    vmem = pl.BlockSpec(memory_space=pltpu.VMEM)
    return pl.pallas_call(
        settle_kernel,
        out_shape=tuple(jax.ShapeDtypeStruct((1,) + grad.shape, grad.dtype) for grad in (dq, dk, dv))
        + (jax.ShapeDtypeStruct(adapters.shape[1:], adapters.dtype),),
        in_specs=[anywhere] * 3 + [vmem],
        out_specs=(anywhere,) * 3 + (vmem,),
        scratch_shapes=[pltpu.VMEM(grad.shape, grad.dtype) for grad in (dq, dk, dv)]
        + [pltpu.SemaphoreType.DMA((3, 4))] * 2,
    )(dq, dk, dv, adapters)


def by_head(shards, queries, keys, values, output_gradient, adapter_hidden, counts, offsets):
    blocks = shards // 2
    total = sum((2 * block + 2 - lower_shard(block)) * T for block in range(blocks))
    bf16, f32 = jnp.bfloat16, jnp.float32
    dma = pltpu.SemaphoreType.DMA
    anywhere = pl.BlockSpec(memory_space=pl.ANY)
    vmem = pl.BlockSpec(memory_space=pltpu.VMEM)
    scalar = pl.BlockSpec(memory_space=pltpu.SMEM)
    dq, dk, dv, adapter = pl.pallas_call(
        functools.partial(head_kernel, shards),
        out_shape=(
            jax.ShapeDtypeStruct((T, HQ * D), bf16),
            jax.ShapeDtypeStruct((T, KEY_VALUE_HEADS * D), bf16),
            jax.ShapeDtypeStruct((T, KEY_VALUE_HEADS * D), bf16),
            jax.ShapeDtypeStruct((2, ADAPTER_RANK, KEY_VALUE_HEADS * D // 2), f32),
        ),
        in_specs=[scalar] * 2 + [anywhere] * 5,
        out_specs=(anywhere, anywhere, anywhere, vmem),
        scratch_shapes=[
            pltpu.VMEM((2, T), f32),
            pltpu.VMEM((shards, 2, T), f32),
            pltpu.VMEM((shards, ADAPTER_RANK, T), bf16),
            pltpu.VMEM((shards, T, D), bf16),
            pltpu.VMEM((shards, T, D), bf16),
            pltpu.VMEM((shards, T, D), bf16),
            pltpu.VMEM((shards, T, D), bf16),
            pltpu.VMEM((D, shards * T), bf16),
            pltpu.VMEM((total, 2 * T), f32),
            pltpu.VMEM((2, shards * T, D), f32),
            pltpu.VMEM((blocks, 2 * T, D), f32),
            pltpu.VMEM((shards, T, D), bf16),
            pltpu.VMEM((shards, T, D), bf16),
            pltpu.VMEM((ADAPTER_RANK, D), f32),
            dma((KEY_VALUE_HEADS, 2)), dma((shards,)),
            dma((KEY_VALUE_HEADS,)), dma((shards,)),
            dma((KEY_VALUE_HEADS,)), dma((shards,)),
            dma((KEY_VALUE_HEADS,)), dma((shards,)),
            dma((KEY_VALUE_HEADS, 2)), dma((shards,)),
            dma((KEY_VALUE_HEADS, 2)), dma((shards,)),
            dma((shards,)), dma((shards,)),
            dma((blocks,)), dma((blocks,)),
            dma((shards,)), dma((HQ,)),
            dma((shards,)), dma((2, KEY_VALUE_HEADS)),
            dma((shards,)), dma((2, KEY_VALUE_HEADS // 2)),
        ],
        compiler_params=pltpu.CompilerParams(
            collective_id=0, has_side_effects=True, vmem_limit_bytes=63 * 1024 * 1024
        ),
    )(counts, offsets, adapter_hidden[0].T, keys[0], values[0], queries[0], output_gradient[0])
    return settle(dq, dk, dv, adapter)


def solution(mesh):
    shards = mesh.shape["context"]
    fits = shards == 2 * KEY_VALUE_HEADS and mesh.shape["fsdp"] == 2
    body = functools.partial(by_head, shards) if fits else local
    in_specs = (
        P("fsdp", "context", None),
        P("fsdp", "context", None),
        P("fsdp", "context", None),
        P("fsdp", "context", None),
        P("fsdp", "context", None),
        P("fsdp", "context"),
        P("fsdp", "context"),
    )
    out_specs = (
        P("fsdp", "context", None),
        P("fsdp", "context", None),
        P("fsdp", "context", None),
        P(None, "fsdp"),
    )
    return jax.shard_map(body, mesh=mesh, in_specs=in_specs, out_specs=out_specs, check_vma=False)
```
